32 devices in a mesh: ctx: 16 (over z, y, x), head: 2 (over core).
Axes of the slice: x: 2, y: 2, z: 4, core: 2. Of those that a mesh axis runs over, the one named last changes fastest.
Arguments:
- q_raw: bfloat16 [8192, 4096], P('ctx', 'head'), may hold values from -60 to 60
- k_raw: bfloat16 [8192, 2048], P('ctx', 'head'), may hold values from -60 to 60
- values: bfloat16 [8192, 2048], P('ctx', 'head'), may hold values from -6 to 6
- d_out: bfloat16 [8192, 4096], P('ctx', 'head'), may hold values from -24 to 24
- doc_ids: int32 [8192], replicated, may hold values from 0 to 7, never falling along the last dimension, each value on 1 to 2048 neighbouring positions
- q_gain: float32 [128], replicated, may hold values from 0.7 to 6.5
- k_gain: float32 [128], replicated, may hold values from 0.7 to 6.5
Outputs:
- q_raw_grad: bfloat16 [8192, 4096], P('ctx', 'head')
- k_raw_grad: bfloat16 [8192, 2048], P('ctx', 'head')
- value_grad: bfloat16 [8192, 2048], P('ctx', 'head')
- q_gain_grad: float32 [128], replicated
- k_gain_grad: float32 [128], replicated
The draws below stay inside these ranges and needn't reach their ends.
All inputs are finite; a program needn't handle non-finite values.
Results may differ from the reference program's by a relative error of at most 0.009.
The reference program's roundings to bfloat16 on the way (of `weights` and `score_grad`) count: a program that leaves them out, or rounds other values in their place, can miss the bound.
Values may be sent and summed in bfloat16 or wider, within the bound.
No kernel may reach another device: no remote copies, remote signals or barrier semaphores. Data moves between devices by JAX's collectives and lax.ppermute only.
A program may use at most 128 MiB of HBM per device.

```python
import math
import jax
import jax.numpy as jnp
import numpy as np
from jax import lax

D_HEAD = 128
Q_HEADS = 32
KV_HEADS = 16
W = 1024
QUERY_SCALE = 168
TOK_DEV = 512
TOKENS = 8192


def key_rows(key):
    drawn = jnp.clip(jax.random.normal(jax.random.fold_in(key, 11), (TOKENS, KV_HEADS, D_HEAD), jnp.float32), -6.0, 6.0)
    return drawn


def draw_k_raw(key, part):
    return key_rows(key).reshape(TOKENS, KV_HEADS * D_HEAD).astype(jnp.bfloat16)


def draw_q_raw(key, part):
    drawn = jnp.clip(jax.random.normal(jax.random.fold_in(key, 21), (TOKENS, Q_HEADS, D_HEAD), jnp.float32), -6.0, 6.0)
    return drawn.reshape(TOKENS, Q_HEADS * D_HEAD).astype(jnp.bfloat16)


def gain_draw(key, salt):
    low_end = 0.7
    high_end = 1.6
    return jax.random.uniform(jax.random.fold_in(key, salt), (D_HEAD,), jnp.float32, low_end, high_end)


def draw_q_gain(key, part):
    return gain_draw(key, 31)


def draw_k_gain(key, part):
    return gain_draw(key, 41)


def levels(own_key, shape, shards, least, high):
    def one(dim, shards_of):
        heights = jax.random.uniform(jax.random.fold_in(jax.random.fold_in(own_key, 6), dim), (shards_of,), jnp.float32, least / len(shards), high / len(shards))
        return jnp.repeat(jnp.exp(heights), shape[dim] // shards_of).reshape((-1,) + (1,) * (len(shape) - dim - 1))

    loudness = one(*shards[0])
    for cut in shards[1:]:
        loudness = loudness * one(*cut)
    return loudness


def split_up(number_of, total, most, slope):
    portions = [(1 << 20) // math.isqrt(standing ** slope) + 1 for standing in range(2, number_of + 1)]
    surplus, given = total - most - (number_of - 1), [1] * (number_of - 1)
    while surplus > 0:
        movable = [i for i in range(number_of - 1) if given[i] < most]
        pool, remaining = sum([portions[i] for i in movable]), surplus
        for i in movable:
            more = min(most - given[i], max(1, remaining * portions[i] // pool), surplus)
            given[i] = given[i] + more
            surplus = surplus - more
    return np.array([most] + given)


def uneven_parts(key, count, total, bound, skew):
    if count == 2:
        one = jax.random.randint(key, (), max(1, total - bound), min(bound, total - 1) + 1)
        return jnp.stack([one, total - one])
    lengths = jnp.asarray(split_up(count, total, bound, skew), jnp.int32)
    pairs = (count - 1) // 2
    source_of, sink = lengths[1:1 + 2 * pairs:2], lengths[2:2 + 2 * pairs:2]
    slack = jnp.minimum(source_of - 1, bound - sink)
    passed = jax.random.randint(jax.random.fold_in(key, 1), (pairs,), 0, 1 << 20) % (slack + 1)
    lengths = lengths.at[1:1 + 2 * pairs:2].set(source_of - passed).at[2:2 + 2 * pairs:2].set(sink + passed)
    return lengths[jax.random.permutation(jax.random.fold_in(key, 2), count)]


def noise(own_key, shape, deviation, reach, pieces=(), kind=jnp.bfloat16):
    result = jax.random.normal(own_key, shape, jnp.float32) * deviation
    if len(pieces) > 0:
        result = levels(own_key, shape, pieces, -0.22, 0.18) * result
    return jnp.clip(result, min=-reach, max=reach).astype(kind)


def setup_inputs(seed: int = 0) -> dict:
    arg_keys = jax.random.split(jax.random.key(seed), 8)
    return {
        "q_raw": draw_q_raw(jax.random.fold_in(arg_keys[7], 71), 0),
        "k_raw": draw_k_raw(jax.random.fold_in(arg_keys[7], 71), 0),
        "values": noise(arg_keys[2], (TOKENS, KV_HEADS * D_HEAD), 1.0, 6.0, ((0, 16), (1, 2))),
        "d_out": noise(arg_keys[3], (TOKENS, Q_HEADS * D_HEAD), 4.0, 24.0, ((0, 16), (1, 2))),
        "doc_ids": jnp.searchsorted(jnp.cumsum(uneven_parts(arg_keys[4], TOKENS // (2 * TOK_DEV), TOKENS, 4 * TOK_DEV, 1)), jnp.arange(TOKENS), side="right").astype(jnp.int32),
        "q_gain": draw_q_gain(jax.random.fold_in(arg_keys[7], 71), 0),
        "k_gain": draw_k_gain(jax.random.fold_in(arg_keys[7], 71), 0),
    }


epsilon = 1e-06

def normalize(raw_data):
    as_float = raw_data.astype(jnp.float32)
    inverse = lax.rsqrt(lax.optimization_barrier(jnp.mean(as_float * as_float, axis=-1, keepdims=True)) + epsilon)
    return (as_float * inverse, inverse)

def norm_back(grad_rows, unit_rows, inverse, gain_vec, factor):
    scaled_grad = grad_rows * (gain_vec * factor)
    raw_grad = inverse * (scaled_grad - unit_rows * lax.optimization_barrier(jnp.mean(scaled_grad * unit_rows, axis=-1, keepdims=True)))
    gain_grad = lax.optimization_barrier(jnp.sum((grad_rows * unit_rows).reshape(-1, unit_rows.shape[-1]), axis=0)) * factor
    return (raw_grad, gain_grad)

def visible(q_pos, q_ids, k_pos, k_ids):
    offset = q_pos[:, None] - k_pos[None, :]
    return (q_ids[:, None] == k_ids[None, :]) & (offset >= 0) & (offset < W)

def row_stats(scores, seen_mask):
    masked = jnp.where(seen_mask, scores, -jnp.inf)
    row_max = lax.optimization_barrier(jnp.max(masked, axis=-1, keepdims=True))
    row_sum = lax.optimization_barrier(jnp.sum(jnp.exp(masked - row_max), axis=-1, keepdims=True))
    log_total = row_max + jnp.log(row_sum)
    softmax = jnp.where(seen_mask, jnp.exp(scores - log_total), 0.0)
    return (softmax, log_total[..., 0])

def reference(q_raw, k_raw, values, d_out, doc_ids, q_gain, k_gain):
    group_size = Q_HEADS // KV_HEADS
    factor = QUERY_SCALE ** (-0.5)
    q_unit, q_inverse = normalize(q_raw.reshape(TOKENS, Q_HEADS, D_HEAD))
    k_unit, k_inverse = normalize(k_raw.reshape(TOKENS, KV_HEADS, D_HEAD))
    q_hat = (q_unit * (q_gain * factor)).astype(jnp.bfloat16).reshape(TOKENS, KV_HEADS, group_size, D_HEAD)
    k_hat = (k_unit * k_gain).astype(jnp.bfloat16)
    front_pad = jnp.zeros((W, KV_HEADS, D_HEAD), jnp.bfloat16)
    k_padded = jnp.concatenate([front_pad, k_hat], axis=0)
    v_padded = jnp.concatenate([front_pad, values.reshape(TOKENS, KV_HEADS, D_HEAD)], axis=0)
    ids_padded = jnp.concatenate([jnp.full((W,), -1, jnp.int32), doc_ids.astype(jnp.int32)])
    grads_out = d_out.reshape(TOKENS, KV_HEADS, group_size, D_HEAD)
    block_rows = 128
    span_rows = W + block_rows

    def block_step(carried, block_index):
        key_acc, value_acc = carried
        row_start = (block_index * block_rows).astype(jnp.int32)
        q_block = lax.dynamic_slice_in_dim(q_hat, row_start, block_rows, 0).astype(jnp.float32)
        g_block = lax.dynamic_slice_in_dim(grads_out, row_start, block_rows, 0).astype(jnp.float32)
        k_block = lax.dynamic_slice_in_dim(k_padded, row_start, span_rows, 0).astype(jnp.float32)
        v_block = lax.dynamic_slice_in_dim(v_padded, row_start, span_rows, 0).astype(jnp.float32)
        q_ids = lax.dynamic_slice_in_dim(doc_ids.astype(jnp.int32), row_start, block_rows, 0)
        k_ids = lax.dynamic_slice_in_dim(ids_padded, row_start, span_rows, 0)
        q_pos = row_start + jnp.arange(block_rows, dtype=jnp.int32)
        k_pos = row_start - W + jnp.arange(span_rows, dtype=jnp.int32)
        seen_mask = visible(q_pos, q_ids, k_pos, k_ids)
        scores = jnp.einsum('tkgd,skd->kgts', q_block, k_block)
        softmax, log_total = row_stats(scores, seen_mask)
        weights = softmax.astype(jnp.bfloat16).astype(jnp.float32)
        attended = jnp.einsum('kgts,skd->tkgd', weights, v_block)
        row_delta = jnp.transpose(lax.optimization_barrier(jnp.sum(g_block * attended, axis=-1)), (1, 2, 0))
        prob_grad = jnp.einsum('tkgd,skd->kgts', g_block, v_block)
        score_grad = (softmax * (prob_grad - row_delta[..., None])).astype(jnp.bfloat16).astype(jnp.float32)
        query_grad = jnp.einsum('kgts,skd->tkgd', score_grad, k_block)
        key_grad = jnp.einsum('kgts,tkgd->skd', score_grad, q_block)
        value_part = jnp.einsum('kgts,tkgd->skd', weights, g_block)
        key_acc = lax.dynamic_update_slice_in_dim(key_acc, lax.dynamic_slice_in_dim(key_acc, row_start, span_rows, 0) + key_grad, row_start, 0)
        value_acc = lax.dynamic_update_slice_in_dim(value_acc, lax.dynamic_slice_in_dim(value_acc, row_start, span_rows, 0) + value_part, row_start, 0)
        return ((key_acc, value_acc), query_grad)
    initial = (jnp.zeros((TOKENS + W, KV_HEADS, D_HEAD), jnp.float32), jnp.zeros((TOKENS + W, KV_HEADS, D_HEAD), jnp.float32))
    (key_acc, value_acc), query_blocks = lax.scan(block_step, initial, jnp.arange(TOKENS // block_rows, dtype=jnp.int32))
    query_grad = query_blocks.reshape(TOKENS, Q_HEADS, D_HEAD)
    key_grad = key_acc[W:]
    value_grad = value_acc[W:]
    q_raw_grad, q_gain_part = norm_back(query_grad, q_unit, q_inverse, q_gain, factor)
    k_raw_grad, k_gain_part = norm_back(key_grad, k_unit, k_inverse, k_gain, 1.0)
    return (q_raw_grad.reshape(TOKENS, Q_HEADS * D_HEAD).astype(jnp.bfloat16), k_raw_grad.reshape(TOKENS, KV_HEADS * D_HEAD).astype(jnp.bfloat16), value_grad.reshape(TOKENS, KV_HEADS * D_HEAD).astype(jnp.bfloat16), q_gain_part / math.sqrt(TOKENS * Q_HEADS), k_gain_part / math.sqrt(TOKENS * KV_HEADS))
```

```python
import functools
import math

import jax
import jax.numpy as jnp
from jax import lax
from jax.experimental import pallas as pl
from jax.experimental.pallas import tpu as pltpu
from jax.sharding import PartitionSpec as P

Q_HEADS = 32
KV_HEADS = 16
W = 1024
QUERY_SCALE = 168
EPS = 1e-06
CHUNKS = (2, 2, 2, 2)
D=128
BF=jnp.bfloat16
F32=jnp.float32
NT=(((1,),(1,)),((),()))
NN=(((1,),(0,)),((),()))
def dotf(a,b,dims):
    return lax.dot_general(a,b,dims,preferred_element_type=F32)

def attn_body(T, rows, halo, par_ref, lo_ref, gq_ref, q_ref, g_ref, own_ref, h1a_ref, h1b_ref, h2_ref,
              qg_ref, own_out, r1_out, r2_out, qgain_ref, kgain_ref,
              ks, vs, kt, s_s, dp_s, ds_s, dk_acc, dv_acc):
    h = pl.program_id(0); i = pl.program_id(1)
    nb = halo // T + 1
    win = halo + T
    @pl.when(i == 0)
    def _():
        def put(ref, at):
            ks[at:at+rows] = ref[:, :D]; vs[at:at+rows] = ref[:, D:]
        put(h2_ref, 0)
        @pl.when(par_ref[0] == 1)
        def _(): put(h1a_ref, rows)
        @pl.when(par_ref[0] == 0)
        def _(): put(h1b_ref, rows)
        put(own_ref, 2*rows)
        kt[...] = ks[...].T
        dk_acc[...] = jnp.zeros_like(dk_acc); dv_acc[...] = jnp.zeros_like(dv_acc)
    @pl.when((i == 0) & (h == 0))
    def _():
        qgain_ref[...] = jnp.zeros_like(qgain_ref); kgain_ref[...] = jnp.zeros_like(kgain_ref)
    w0 = pl.multiple_of(i * T, T)
    def cols(ref):
        return jnp.concatenate([ref[:, :D].T, ref[:, D:].T], axis=1)
    gq = gq_ref[...]
    qf = cols(q_ref).astype(F32)
    q_inv = lax.rsqrt(jnp.mean(qf*qf, axis=0, keepdims=True) + 1e-6)
    q_unit = qf * q_inv
    qt = (q_unit * gq).astype(BF)
    gt = cols(g_ref)
    lo = lo_ref[...] - i*T
    lo = jnp.concatenate([lo, lo], axis=1)
    iota = lax.broadcasted_iota(jnp.int32, (T, 2*T), 0)
    lane = lax.broadcasted_iota(jnp.int32, (T, 2*T), 1)
    tok = jnp.where(lane >= T, lane - T, lane)
    def fold(x, op):
        return op(x.reshape(T//8, 8, 2*T), axis=0)
    m8 = None
    for kb in range(nb):
        s = dotf(ks[pl.ds(w0 + kb*T, T), :], qt, NN)
        see = iota >= lo - kb*T
        if kb == nb-1: see = see & (iota <= tok)
        s = jnp.where(see, s, -1e30)
        s_s[kb*T:(kb+1)*T] = s
        f = fold(s, jnp.max)
        m8 = f if m8 is None else jnp.maximum(m8, f)
    m = jnp.max(m8, axis=0, keepdims=True)
    l8 = None
    for kb in range(nb):
        e = jnp.exp(s_s[kb*T:(kb+1)*T] - m)
        s_s[kb*T:(kb+1)*T] = e
        f = fold(e, jnp.sum)
        l8 = f if l8 is None else l8 + f
        dp_s[kb*T:(kb+1)*T] = dotf(vs[pl.ds(w0 + kb*T, T), :], gt, NN)
    inv_l = 1.0 / jnp.sum(l8, axis=0, keepdims=True)
    d8 = None
    for kb in range(nb):
        w = (s_s[kb*T:(kb+1)*T] * inv_l).astype(BF)
        f = fold(w.astype(F32) * dp_s[kb*T:(kb+1)*T], jnp.sum)
        d8 = f if d8 is None else d8 + f
        at = pl.ds(w0 + kb*T, T)
        dv_acc[at, :] = dv_acc[at, :] + dotf(w, gt, NT)
    delta = jnp.sum(d8, axis=0, keepdims=True)
    for kb in range(nb):
        p = s_s[kb*T:(kb+1)*T] * inv_l
        ds = (p * (dp_s[kb*T:(kb+1)*T] - delta)).astype(BF)
        ds_s[kb*T:(kb+1)*T] = ds
        at = pl.ds(w0 + kb*T, T)
        dk_acc[at, :] = dk_acc[at, :] + dotf(ds, qt, NT)
    dq = dotf(kt[:, pl.ds(w0, win)], ds_s[...], NN)
    qgain_ref[...] += dq * q_unit
    up = dq * gq
    mean = jnp.mean(up * q_unit, axis=0, keepdims=True)
    qr = (q_inv * (up - q_unit * mean)).astype(BF)
    qg_ref[:, :D] = qr[:, :T].T
    qg_ref[:, D:] = qr[:, T:].T
    @pl.when(i == rows // T - 1)
    def _():
        own_out[:, :D] = dk_acc[2*rows:]; own_out[:, D:] = dv_acc[2*rows:]
        r1_out[:, :D] = dk_acc[rows:2*rows].astype(BF); r1_out[:, D:] = dv_acc[rows:2*rows].astype(BF)
        r2_out[:, :D] = dk_acc[:rows].astype(BF); r2_out[:, D:] = dv_acc[:rows].astype(BF)
        kgain_ref[...] += jnp.sum((dk_acc[...] * ks[...].astype(F32)).reshape(-1, 8, D), axis=0)

def attn(par, lo, gq, q, g, own, h1a, h1b, h2, off, hc, qg_prev=None):
    rows = q.shape[0]; T = 128; halo = 2*rows
    win = halo + T
    kvs = pl.BlockSpec((rows, 2*D), lambda h, i: (0, h))
    in_specs=[pl.BlockSpec(memory_space=pltpu.SMEM),
              pl.BlockSpec((1,T), lambda h,i:(0,i)),
              pl.BlockSpec((D,1), lambda h,i:(0,0)),
              pl.BlockSpec((T,2*D), lambda h,i:(i,off+h)),
              pl.BlockSpec((T,2*D), lambda h,i:(i,off+h)),
              kvs,kvs,kvs,kvs]
    args=[par,lo,gq,q,g,own,h1a,h1b,h2]
    body = functools.partial(attn_body, T, rows, halo)
    alias={}
    if qg_prev is not None:
        in_specs.append(pl.BlockSpec(memory_space=pl.ANY)); args.append(qg_prev); alias={9:0}
        inner = body
        body = lambda *r: inner(*r[:9], *r[10:])
    return pl.pallas_call(body, grid=(hc, rows//T), in_specs=in_specs,
        out_specs=[pl.BlockSpec((T,2*D), lambda h,i:(i,off+h)), kvs,kvs,kvs,
                   pl.BlockSpec((D,2*T), lambda h,i:(0,0)), pl.BlockSpec((8,D), lambda h,i:(0,0))],
        out_shape=[jax.ShapeDtypeStruct(q.shape,BF), jax.ShapeDtypeStruct((rows,hc*2*D),F32),
                   jax.ShapeDtypeStruct((rows,hc*2*D),BF), jax.ShapeDtypeStruct((rows,hc*2*D),BF),
                   jax.ShapeDtypeStruct((D,2*T),F32), jax.ShapeDtypeStruct((8,D),F32)],
        scratch_shapes=[pltpu.VMEM((3*rows,D),BF),pltpu.VMEM((3*rows,D),BF),pltpu.VMEM((D,3*rows),BF),
            pltpu.VMEM((win,2*T),F32),pltpu.VMEM((win,2*T),F32),pltpu.VMEM((win,2*T),BF),
            pltpu.VMEM((3*rows,D),F32),pltpu.VMEM((3*rows,D),F32)],
        input_output_aliases=alias,
        compiler_params=pltpu.CompilerParams(dimension_semantics=("arbitrary","arbitrary"), vmem_limit_bytes=40*1024*1024),
        name="attn_grad")(*args)


def pack_body(hc, k_ref, v_ref, gain_ref, out_ref):
    for h in range(hc):
        k = k_ref[:, h*D:(h+1)*D].astype(F32)
        inv = lax.rsqrt(jnp.mean(k*k, axis=1, keepdims=True) + EPS)
        out_ref[:, 2*h*D:(2*h+1)*D] = (k * inv * gain_ref[...]).astype(BF)
        out_ref[:, (2*h+1)*D:(2*h+2)*D] = v_ref[:, h*D:(h+1)*D]


def pack(k_raw, values, k_gain, off, hc):
    rows = k_raw.shape[0]
    cb = [pl.BlockSpec((rows, D), lambda h: (0, off + h))] * 2
    return pl.pallas_call(
        functools.partial(pack_body, 1), grid=(hc,),
        in_specs=cb + [pl.BlockSpec((1, D), lambda h: (0, 0))],
        out_specs=pl.BlockSpec((rows, 2*D), lambda h: (0, h)),
        out_shape=jax.ShapeDtypeStruct((rows, hc*2*D), BF),
        name="pack_kv")(k_raw, values, k_gain)


def finish_body(par_ref, own_ref, x_ref, y_ref, k_ref, gain_ref, *refs):
    kg_ref, vg_ref = refs[-2:]
    even = jnp.where(par_ref[0] == 0, 1.0, 0.0)
    t = own_ref[...] + y_ref[...].astype(F32) + x_ref[...].astype(F32) * even
    vg_ref[...] = t[:, D:].astype(BF)
    k = k_ref[...].astype(F32)
    inv = lax.rsqrt(jnp.mean(k*k, axis=1, keepdims=True) + EPS)
    unit = k * inv
    up = t[:, :D] * gain_ref[...]
    kg_ref[...] = (inv * (up - unit * jnp.mean(up * unit, axis=1, keepdims=True))).astype(BF)


def finish(par, own, x, y, k_raw, k_gain, off, hc, prev):
    rows = own.shape[0]
    kvs = pl.BlockSpec((rows, 2*D), lambda h: (0, h))
    cb = pl.BlockSpec((rows, D), lambda h: (0, off + h))
    in_specs = [pl.BlockSpec(memory_space=pltpu.SMEM), kvs, kvs, kvs, cb, pl.BlockSpec((1, D), lambda h: (0, 0))]
    args = [par, own, x, y, k_raw, k_gain]
    alias = {}
    if prev is not None:
        in_specs += [pl.BlockSpec(memory_space=pl.ANY)] * 2
        args += list(prev)
        alias = {6: 0, 7: 1}
    return pl.pallas_call(
        finish_body, grid=(hc,), in_specs=in_specs, out_specs=[cb, cb],
        out_shape=[jax.ShapeDtypeStruct(k_raw.shape, BF)] * 2,
        input_output_aliases=alias, name="finish_kv")(*args)


def on_device(q_raw, k_raw, values, d_out, doc_ids, q_gain, k_gain):
    rows = q_raw.shape[0]
    kv_local = k_raw.shape[1] // D
    count = lax.axis_size("ctx")
    assert 2 * rows == W and count % 2 == 0 and q_raw.shape[1] == 2 * k_raw.shape[1]
    chunks = CHUNKS if kv_local == sum(CHUNKS) else (1,) * kv_local
    factor = QUERY_SCALE ** (-0.5)
    me = lax.axis_index("ctx")
    par = (me % 2).astype(jnp.int32).reshape(1)
    onward = [(i, i + 2) for i in range(count - 2)]
    back = [(i + 2, i) for i in range(count - 2)]
    swap = [(i, i ^ 1) for i in range(count)]
    up = [(i, i + 1) for i in range(0, count, 2)]
    down = [(i + 1, i) for i in range(0, count, 2)]

    gk = k_gain.reshape(1, D)
    own, far, near_a, near_b = [], [], [], []
    off = 0
    for hc in chunks:
        own.append(pack(k_raw, values, gk, off, hc))
        off += hc
    for c in range(len(chunks)):
        far.append(lax.ppermute(own[c], "ctx", onward))
        near_a.append(lax.ppermute(own[c], "ctx", up))
    for c in range(len(chunks)):
        near_b.append(lax.ppermute(far[c], "ctx", down))

    padded = jnp.concatenate([jnp.full((W,), -1, jnp.int32), doc_ids])
    span_ids = lax.dynamic_slice_in_dim(padded, me * rows, W + rows)
    q_ids = span_ids[W:]
    first = jnp.sum((span_ids[:, None] < q_ids[None, :]).astype(jnp.int32), axis=0)
    lo = jnp.maximum(first, jnp.arange(1, rows + 1, dtype=jnp.int32)).reshape(1, rows)
    gq = (q_gain * factor).reshape(D, 1)

    qg = None
    mine, r1, r2, qs, kss = [], [], [], [], []
    off = 0
    for c, hc in enumerate(chunks):
        qg, o, a, b, s, t = attn(par, lo, gq, q_raw, d_out, own[c], near_a[c], near_b[c], far[c], off, hc, qg)
        mine.append(o); r1.append(a); r2.append(b); qs.append(s); kss.append(t)
        off += hc
    q_part = jnp.sum(sum(qs), axis=1) * factor
    k_part = jnp.sum(sum(kss), axis=0) / k_gain
    gains = lax.psum(jnp.stack([q_part, k_part]), ("ctx", "head"))

    out = None
    off = 0
    for c, hc in enumerate(chunks):
        x = lax.ppermute(r1[c], "ctx", swap)
        both = (r2[c].astype(F32) + x.astype(F32)).astype(BF)
        y = lax.ppermute(jnp.where(par[0] == 1, both, r2[c]), "ctx", back)
        out = finish(par, mine[c], x, y, k_raw, gk, off, hc, out)
        off += hc
    total = rows * count
    return (qg, out[0], out[1], gains[0] / math.sqrt(total * Q_HEADS), gains[1] / math.sqrt(total * KV_HEADS))


def solution(mesh):
    split = P("ctx", "head")
    return jax.shard_map(
        on_device,
        mesh=mesh,
        in_specs=(split, split, split, split, P(), P(), P()),
        out_specs=(split, split, split, P(), P()),
        check_vma=False,
    )
```

```python
import functools
import math

import jax
import jax.numpy as jnp
from jax import lax
from jax.experimental import pallas as pl
from jax.experimental.pallas import tpu as pltpu
from jax.sharding import PartitionSpec as P

Q_HEADS = 32
KV_HEADS = 16
W = 1024
QUERY_SCALE = 168
EPS = 1e-06
CHUNKS = (2, 2, 2, 2)
GATE = 1
GATE2 = 1
D=128
BF=jnp.bfloat16
F32=jnp.float32
NT=(((1,),(1,)),((),()))
NN=(((1,),(0,)),((),()))
ORDER="half"
ACC="rmw"
def dotf(a,b,dims):
    return lax.dot_general(a,b,dims,preferred_element_type=F32)

def attn_body(T, rows, par_ref, lo_ref, gq_ref, q_ref, g_ref, own_ref, h1a_ref, h1b_ref, h2_ref,
              qg_ref, own_out, r1_out, r2_out, qgain_ref, kgain_ref,
              near, kt, s_s, dp_s, w_s, ds_s, dk_acc, dv_acc):
    h = pl.program_id(0)
    nq = rows // T
    nb = 2 * nq + 1
    @pl.when(par_ref[0] == 1)
    def _(): near[...] = h1a_ref[...]
    @pl.when(par_ref[0] == 0)
    def _(): near[...] = h1b_ref[...]
    @pl.when(h == 0)
    def _():
        qgain_ref[...] = jnp.zeros_like(qgain_ref); kgain_ref[...] = jnp.zeros_like(kgain_ref)
    kv = [h2_ref, near, own_ref]
    def kk(j): return kv[j//nq][(j%nq)*T:(j%nq+1)*T, :D]
    def vv(j): return kv[j//nq][(j%nq)*T:(j%nq+1)*T, D:]
    for p in range(3):
        kt[:, p*rows:(p+1)*rows] = kv[p][:, :D].T
    gq = gq_ref[...]
    iota = lax.broadcasted_iota(jnp.int32, (T, 2*T), 0)
    lane = lax.broadcasted_iota(jnp.int32, (T, 2*T), 1)
    tok = jnp.where(lane >= T, lane - T, lane)
    def fold(x, op):
        return op(x.reshape(T//8, 8, 2*T), axis=0)
    st = [dict() for _ in range(nq)]
    def sl(kb): return slice(kb*T, (kb+1)*T)
    def p0(i):
        t = st[i]
        r = slice(i*T, (i+1)*T)
        qf = jnp.concatenate([q_ref[r, :D].T, q_ref[r, D:].T], axis=1).astype(F32)
        t["inv"] = lax.rsqrt(jnp.mean(qf*qf, axis=0, keepdims=True) + 1e-6)
        unit = qf * t["inv"]
        t["unit"] = unit
        t["qt"] = (unit * gq).astype(BF)
        t["gt"] = jnp.concatenate([g_ref[r, :D].T, g_ref[r, D:].T], axis=1)
        lo = lo_ref[:, r] - i*T
        t["lo"] = jnp.concatenate([lo, lo], axis=1)
        yield
    def p1(i):
        t = st[i]; b = i % 2; m8 = None
        for kb in range(nb):
            s = dotf(kk(i+kb), t["qt"], NN)
            see = iota >= t["lo"] - kb*T
            if kb == nb-1: see = see & (iota <= tok)
            s = jnp.where(see, s, -1e30)
            s_s[b, sl(kb)] = s
            f = fold(s, jnp.max)
            m8 = f if m8 is None else jnp.maximum(m8, f)
            yield
        t["m"] = jnp.max(m8, axis=0, keepdims=True)
    def p2(i):
        t = st[i]; b = i % 2; l8 = None
        for kb in range(nb):
            e = jnp.exp(s_s[b, sl(kb)] - t["m"])
            s_s[b, sl(kb)] = e
            f = fold(e, jnp.sum)
            l8 = f if l8 is None else l8 + f
            dp_s[b, sl(kb)] = dotf(vv(i+kb), t["gt"], NN)
            yield
        t["il"] = 1.0 / jnp.sum(l8, axis=0, keepdims=True)
    def acc(ref, first, j, val):
        r = slice(j*T, (j+1)*T)
        if first: ref[r] = val
        else: ref[r] = ref[r] + val
    def p3(i):
        t = st[i]; b = i % 2; d8 = None
        for kb in range(nb):
            w = (s_s[b, sl(kb)] * t["il"]).astype(BF)
            f = fold(w.astype(F32) * dp_s[b, sl(kb)], jnp.sum)
            d8 = f if d8 is None else d8 + f
            if ACC == "rmw":
                acc(dv_acc, i == 0 or kb == nb-1, i+kb, dotf(w, t["gt"], NT))
            yield
        t["delta"] = jnp.sum(d8, axis=0, keepdims=True)
    def p4(i):
        t = st[i]; b = i % 2
        for kb in range(nb):
            p = s_s[b, sl(kb)] * t["il"]
            ds = (p * (dp_s[b, sl(kb)] - t["delta"])).astype(BF)
            ds_s[b, sl(kb)] = ds
            acc(dk_acc, i == 0 or kb == nb-1, i+kb, dotf(ds, t["qt"], NT))
            yield
    def p5(i):
        t = st[i]; b = i % 2
        dq = dotf(kt[:, i*T:(i+nb)*T], ds_s[b], NN)
        qgain_ref[...] += dq * t["unit"]
        up = dq * gq
        mean = jnp.mean(up * t["unit"], axis=0, keepdims=True)
        qr = (t["inv"] * (up - t["unit"] * mean)).astype(BF)
        r = slice(i*T, (i+1)*T)
        qg_ref[r, :D] = qr[:, :T].T
        qg_ref[r, D:] = qr[:, T:].T
        yield
    def run(*gens):
        gens = list(gens)
        while gens:
            for g in list(gens):
                try: next(g)
                except StopIteration: gens.remove(g)
    def chain(*gs):
        for g in gs: yield from g
    if ORDER == "seq":
        for i in range(nq):
            run(chain(p0(i), p1(i), p2(i), p3(i), p4(i), p5(i)))
    elif ORDER == "half":
        run(chain(p0(0), p1(0), p2(0)))
        for i in range(nq):
            nxt = [chain(p0(i+1), p1(i+1), p2(i+1))] if i+1 < nq else []
            run(chain(p3(i), p4(i), p5(i)), *nxt)
    elif ORDER == "pair":
        for i in range(0, nq, 2):
            run(chain(p0(i), p1(i), p2(i), p3(i), p4(i), p5(i)), chain(p0(i+1), p1(i+1), p2(i+1), p3(i+1), p4(i+1), p5(i+1)))
    own_out[:, :D] = dk_acc[2*rows:]; own_out[:, D:] = dv_acc[2*rows:]
    r1_out[:, :D] = dk_acc[rows:2*rows].astype(BF); r1_out[:, D:] = dv_acc[rows:2*rows].astype(BF)
    r2_out[:, :D] = dk_acc[:rows].astype(BF); r2_out[:, D:] = dv_acc[:rows].astype(BF)
    kg = None
    for p in range(3):
        f = jnp.sum((dk_acc[p*rows:(p+1)*rows] * kv[p][:, :D].astype(F32)).reshape(-1, 8, D), axis=0)
        kg = f if kg is None else kg + f
    kgain_ref[...] += kg

def attn(par, lo, gq, q, g, own, h1a, h1b, h2, off, hc, qg_prev=None):
    rows = q.shape[0]; T = 128
    win = 2*rows + T
    kvs = pl.BlockSpec((rows, 2*D), lambda h: (0, h))
    qs = pl.BlockSpec((rows, 2*D), lambda h: (0, off+h))
    in_specs=[pl.BlockSpec(memory_space=pltpu.SMEM),
              pl.BlockSpec((1,rows), lambda h:(0,0)),
              pl.BlockSpec((D,1), lambda h:(0,0)),
              qs, qs, kvs,kvs,kvs,kvs]
    args=[par,lo,gq,q,g,own,h1a,h1b,h2]
    body = functools.partial(attn_body, T, rows)
    alias={}
    if qg_prev is not None:
        in_specs.append(pl.BlockSpec(memory_space=pl.ANY)); args.append(qg_prev); alias={9:0}
        inner = body
        body = lambda *r: inner(*r[:9], *r[10:])
    return pl.pallas_call(body, grid=(hc,), in_specs=in_specs,
        out_specs=[qs, kvs,kvs,kvs,
                   pl.BlockSpec((D,2*T), lambda h:(0,0)), pl.BlockSpec((8,D), lambda h:(0,0))],
        out_shape=[jax.ShapeDtypeStruct(q.shape,BF), jax.ShapeDtypeStruct((rows,hc*2*D),F32),
                   jax.ShapeDtypeStruct((rows,hc*2*D),BF), jax.ShapeDtypeStruct((rows,hc*2*D),BF),
                   jax.ShapeDtypeStruct((D,2*T),F32), jax.ShapeDtypeStruct((8,D),F32)],
        scratch_shapes=[pltpu.VMEM((rows,2*D),BF),pltpu.VMEM((D,3*rows),BF),
            pltpu.VMEM((2,win,2*T),F32),pltpu.VMEM((2,win,2*T),F32),pltpu.VMEM((16,128),BF),pltpu.VMEM((2,win,2*T),BF),
            pltpu.VMEM((3*rows,D),F32),pltpu.VMEM((3*rows,D),F32)],
        input_output_aliases=alias,
        cost_estimate=pl.CostEstimate(flops=hc*6*10**9, bytes_accessed=hc*rows*D*24, transcendentals=0),
        compiler_params=pltpu.CompilerParams(dimension_semantics=("arbitrary",), vmem_limit_bytes=60*1024*1024),
        name="attn_grad")(*args)


def pack_body(chunks, k_ref, v_ref, gain_ref, *outs):
    h = pl.program_id(0)
    k = k_ref[...].astype(F32)
    inv = lax.rsqrt(jnp.mean(k*k, axis=1, keepdims=True) + EPS)
    k = (k * inv * gain_ref[...]).astype(BF)
    at = 0
    for hc, out in zip(chunks, outs):
        @pl.when((h >= at) & (h < at + hc))
        def _(out=out):
            out[:, :D] = k
            out[:, D:] = v_ref[...]
        at += hc


def pack(k_raw, values, k_gain, off, chunks):
    rows = k_raw.shape[0]
    cb = [pl.BlockSpec((rows, D), lambda h: (0, off + h))] * 2
    outs, at = [], 0
    for hc in chunks:
        outs.append(pl.BlockSpec((rows, 2*D), lambda h, at=at, hc=hc: (0, jnp.clip(h - at, 0, hc - 1))))
        at += hc
    return pl.pallas_call(
        functools.partial(pack_body, chunks), grid=(at,),
        in_specs=cb + [pl.BlockSpec((1, D), lambda h: (0, 0))],
        out_specs=outs,
        out_shape=[jax.ShapeDtypeStruct((rows, hc*2*D), BF) for hc in chunks],
        cost_estimate=pl.CostEstimate(flops=at*10**9, bytes_accessed=at*rows*D*8, transcendentals=0),
        name="pack_kv")(k_raw, values, k_gain)


def finish_body(par_ref, own_ref, x_ref, y_ref, k_ref, gain_ref, *refs):
    kg_ref, vg_ref = refs[-2:]
    even = jnp.where(par_ref[0] == 0, 1.0, 0.0)
    t = own_ref[...] + y_ref[...].astype(F32) + x_ref[...].astype(F32) * even
    vg_ref[...] = t[:, D:].astype(BF)
    k = k_ref[...].astype(F32)
    inv = lax.rsqrt(jnp.mean(k*k, axis=1, keepdims=True) + EPS)
    unit = k * inv
    up = t[:, :D] * gain_ref[...]
    kg_ref[...] = (inv * (up - unit * jnp.mean(up * unit, axis=1, keepdims=True))).astype(BF)


def finish(par, own, x, y, k_raw, k_gain, off, hc, prev):
    rows = own.shape[0]
    kvs = pl.BlockSpec((rows, 2*D), lambda h: (0, h))
    cb = pl.BlockSpec((rows, D), lambda h: (0, off + h))
    in_specs = [pl.BlockSpec(memory_space=pltpu.SMEM), kvs, kvs, kvs, cb, pl.BlockSpec((1, D), lambda h: (0, 0))]
    args = [par, own, x, y, k_raw, k_gain]
    alias = {}
    if prev is not None:
        in_specs += [pl.BlockSpec(memory_space=pl.ANY)] * 2
        args += list(prev)
        alias = {6: 0, 7: 1}
    return pl.pallas_call(
        finish_body, grid=(hc,), in_specs=in_specs, out_specs=[cb, cb],
        out_shape=[jax.ShapeDtypeStruct(k_raw.shape, BF)] * 2,
        cost_estimate=pl.CostEstimate(flops=hc*10**9, bytes_accessed=hc*rows*D*8, transcendentals=0),
        input_output_aliases=alias, name="finish_kv")(*args)


def move(value, pairs, name):
    with jax.named_scope(name):
        return lax.ppermute(value, "ctx", pairs)


def after(value, *others):
    return lax.optimization_barrier((value,) + others)[0]


def sum_all(x):
    for name in ("head", "ctx"):
        count = lax.axis_size(name)
        if count & (count - 1):
            x = lax.psum(x, name)
            continue
        step = 1
        while step < count:
            x = x + lax.ppermute(x, name, [(i, i ^ step) for i in range(count)])
            step *= 2
    return x


def on_device(q_raw, k_raw, values, d_out, doc_ids, q_gain, k_gain):
    rows = q_raw.shape[0]
    kv_local = k_raw.shape[1] // D
    count = lax.axis_size("ctx")
    assert 2 * rows == W and count % 2 == 0 and q_raw.shape[1] == 2 * k_raw.shape[1]
    chunks = CHUNKS if kv_local == sum(CHUNKS) else (1,) * kv_local
    factor = QUERY_SCALE ** (-0.5)
    me = lax.axis_index("ctx")
    par = (me % 2).astype(jnp.int32).reshape(1)
    onward = [(i, i + 2) for i in range(count - 2)]
    back = [(i + 2, i) for i in range(count - 2)]
    swap = [(i, i ^ 1) for i in range(count)]
    up = [(i, i + 1) for i in range(0, count, 2)]
    down = [(i + 1, i) for i in range(0, count, 2)]

    gk = k_gain.reshape(1, D)
    n = len(chunks)
    own = list(pack(k_raw, values, gk, 0, chunks[:1])) + list(pack(k_raw, values, gk, chunks[0], chunks[1:]))
    far, near_a, near_b = [None] * n, [None] * n, [None] * n
    for c in range(n):
        far[c] = move(own[c], onward, f"far{c}")
        near_a[c] = move(own[c], up, f"up{c}")
        near_b[c] = move(far[c], down, f"relay{c}")

    padded = jnp.concatenate([jnp.full((W,), -1, jnp.int32), doc_ids])
    span_ids = lax.dynamic_slice_in_dim(padded, me * rows, W + rows)
    q_ids = span_ids[W:]
    first = jnp.sum((span_ids[:, None] < q_ids[None, :]).astype(jnp.int32), axis=0)
    lo = jnp.maximum(first, jnp.arange(1, rows + 1, dtype=jnp.int32)).reshape(1, rows)
    gq = (q_gain * factor).reshape(D, 1)

    offs = [sum(chunks[:c]) for c in range(n)]
    qg = None
    mine, r1, r2, qs, kss, xs, ys = [], [], [], [], [], [], []

    def give(c, last):
        t = after(r2[c], last)
        both = (t.astype(F32) + xs[c].astype(F32)).astype(BF)
        t = jnp.where(par[0] == 1, both, t)
        ys.append(move(t, back, f"ret{c}"))
        return t

    tok = par
    for c in range(n):
        if c >= 2:
            tok = after(tok, give(c - 2, kss[c - 1]))
        if c >= 3:
            tok, ys[c - 3] = lax.optimization_barrier((tok, ys[c - 3]))
        qg, o, a, b, s, t = attn(tok, lo, gq, q_raw, d_out, own[c], near_a[c], near_b[c], far[c], offs[c], chunks[c], qg)
        mine.append(o); r1.append(a); r2.append(b); qs.append(s); kss.append(t)
        xs.append(move(r1[c], swap, f"swap{c}"))
    out = None
    give(n - 2, kss[n - 1])
    for c in range(n - 2):
        out = finish(after(par, ys[n - 2] if False else kss[n - 1]), mine[c], xs[c], ys[c], k_raw, gk, offs[c], chunks[c], out)
    t = give(n - 1, kss[n - 1] if GATE == 0 or out is None else out[0])
    q_part = jnp.sum(sum(qs), axis=1) * factor
    k_part = jnp.sum(sum(kss), axis=0) / k_gain
    gains = jnp.stack([q_part, k_part])
    if GATE2:
        gains = after(gains, t)
    gains = sum_all(gains)
    for c in range(n - 2, n):
        out = finish(par, mine[c], xs[c], ys[c], k_raw, gk, offs[c], chunks[c], out)
    total = rows * count
    return (qg, out[0], out[1], gains[0] / math.sqrt(total * Q_HEADS), gains[1] / math.sqrt(total * KV_HEADS))


def solution(mesh):
    split = P("ctx", "head")
    return jax.shard_map(
        on_device,
        mesh=mesh,
        in_specs=(split, split, split, split, P(), P(), P()),
        out_specs=(split, split, split, P(), P()),
        check_vma=False,
    )
```

```python
import functools
import math

import jax
import jax.numpy as jnp
from jax import lax
from jax.experimental import pallas as pl
from jax.experimental.pallas import tpu as pltpu
from jax.sharding import PartitionSpec as P

Q_HEADS = 32
KV_HEADS = 16
W = 1024
QUERY_SCALE = 168
EPS = 1e-06
CHUNKS = (2, 2, 3, 1)
GATE = 1
GATE2 = 0
EARLY = 2
DIRECT = 0
D=128
BF=jnp.bfloat16
F32=jnp.float32
NT=(((1,),(1,)),((),()))
NN=(((1,),(0,)),((),()))
ORDER="half"
ACC="rmw"
def dotf(a,b,dims):
    return lax.dot_general(a,b,dims,preferred_element_type=F32)

def attn_body(T, rows, par_ref, lo_ref, gq_ref, q_ref, g_ref, own_ref, h1a_ref, h1b_ref, h2_ref,
              qg_ref, own_out, r1_out, r2_out, qgain_ref, kgain_ref,
              near, kt, s_s, dp_s, w_s, ds_s, dk_acc, dv_acc):
    h = pl.program_id(0)
    nq = rows // T
    nb = 2 * nq + 1
    @pl.when(par_ref[0] == 1)
    def _(): near[...] = h1a_ref[...]
    @pl.when(par_ref[0] == 0)
    def _(): near[...] = h1b_ref[...]
    @pl.when(h == 0)
    def _():
        qgain_ref[...] = jnp.zeros_like(qgain_ref); kgain_ref[...] = jnp.zeros_like(kgain_ref)
    kv = [h2_ref, near, own_ref]
    def kk(j): return kv[j//nq][(j%nq)*T:(j%nq+1)*T, :D]
    def vv(j): return kv[j//nq][(j%nq)*T:(j%nq+1)*T, D:]
    for p in range(3):
        kt[:, p*rows:(p+1)*rows] = kv[p][:, :D].T
    gq = gq_ref[...]
    iota = lax.broadcasted_iota(jnp.int32, (T, 2*T), 0)
    lane = lax.broadcasted_iota(jnp.int32, (T, 2*T), 1)
    tok = jnp.where(lane >= T, lane - T, lane)
    def fold(x, op):
        return op(x.reshape(T//8, 8, 2*T), axis=0)
    st = [dict() for _ in range(nq)]
    def sl(kb): return slice(kb*T, (kb+1)*T)
    def p0(i):
        t = st[i]
        r = slice(i*T, (i+1)*T)
        qf = jnp.concatenate([q_ref[r, :D].T, q_ref[r, D:].T], axis=1).astype(F32)
        t["inv"] = lax.rsqrt(jnp.mean(qf*qf, axis=0, keepdims=True) + 1e-6)
        unit = qf * t["inv"]
        t["unit"] = unit
        t["qt"] = (unit * gq).astype(BF)
        t["gt"] = jnp.concatenate([g_ref[r, :D].T, g_ref[r, D:].T], axis=1)
        lo = lo_ref[:, r] - i*T
        t["lo"] = jnp.concatenate([lo, lo], axis=1)
        yield
    def p1(i):
        t = st[i]; b = i % 2; m8 = None
        for kb in range(nb):
            s = dotf(kk(i+kb), t["qt"], NN)
            see = iota >= t["lo"] - kb*T
            if kb == nb-1: see = see & (iota <= tok)
            s = jnp.where(see, s, -1e30)
            s_s[b, sl(kb)] = s
            f = fold(s, jnp.max)
            m8 = f if m8 is None else jnp.maximum(m8, f)
            yield
        t["m"] = jnp.max(m8, axis=0, keepdims=True)
    def p2(i):
        t = st[i]; b = i % 2; l8 = None
        for kb in range(nb):
            e = jnp.exp(s_s[b, sl(kb)] - t["m"])
            s_s[b, sl(kb)] = e
            f = fold(e, jnp.sum)
            l8 = f if l8 is None else l8 + f
            dp_s[b, sl(kb)] = dotf(vv(i+kb), t["gt"], NN)
            yield
        t["il"] = 1.0 / jnp.sum(l8, axis=0, keepdims=True)
    def acc(ref, first, j, val):
        r = slice(j*T, (j+1)*T)
        if first: ref[r] = val
        else: ref[r] = ref[r] + val
    def p3(i):
        t = st[i]; b = i % 2; d8 = None
        for kb in range(nb):
            w = (s_s[b, sl(kb)] * t["il"]).astype(BF)
            f = fold(w.astype(F32) * dp_s[b, sl(kb)], jnp.sum)
            d8 = f if d8 is None else d8 + f
            if ACC == "rmw":
                acc(dv_acc, i == 0 or kb == nb-1, i+kb, dotf(w, t["gt"], NT))
            yield
        t["delta"] = jnp.sum(d8, axis=0, keepdims=True)
    def p4(i):
        t = st[i]; b = i % 2
        for kb in range(nb):
            p = s_s[b, sl(kb)] * t["il"]
            ds = (p * (dp_s[b, sl(kb)] - t["delta"])).astype(BF)
            ds_s[b, sl(kb)] = ds
            acc(dk_acc, i == 0 or kb == nb-1, i+kb, dotf(ds, t["qt"], NT))
            yield
    def p5(i):
        t = st[i]; b = i % 2
        dq = dotf(kt[:, i*T:(i+nb)*T], ds_s[b], NN)
        qgain_ref[...] += dq * t["unit"]
        up = dq * gq
        mean = jnp.mean(up * t["unit"], axis=0, keepdims=True)
        qr = (t["inv"] * (up - t["unit"] * mean)).astype(BF)
        r = slice(i*T, (i+1)*T)
        qg_ref[r, :D] = qr[:, :T].T
        qg_ref[r, D:] = qr[:, T:].T
        yield
    def run(*gens):
        gens = list(gens)
        while gens:
            for g in list(gens):
                try: next(g)
                except StopIteration: gens.remove(g)
    def chain(*gs):
        for g in gs: yield from g
    if ORDER == "seq":
        for i in range(nq):
            run(chain(p0(i), p1(i), p2(i), p3(i), p4(i), p5(i)))
    elif ORDER == "half":
        run(chain(p0(0), p1(0), p2(0)))
        for i in range(nq):
            nxt = [chain(p0(i+1), p1(i+1), p2(i+1))] if i+1 < nq else []
            run(chain(p3(i), p4(i), p5(i)), *nxt)
    elif ORDER == "pair":
        for i in range(0, nq, 2):
            run(chain(p0(i), p1(i), p2(i), p3(i), p4(i), p5(i)), chain(p0(i+1), p1(i+1), p2(i+1), p3(i+1), p4(i+1), p5(i+1)))
    own_out[:, :D] = dk_acc[2*rows:]; own_out[:, D:] = dv_acc[2*rows:]
    r1_out[:, :D] = dk_acc[rows:2*rows].astype(BF); r1_out[:, D:] = dv_acc[rows:2*rows].astype(BF)
    r2_out[:, :D] = dk_acc[:rows].astype(BF); r2_out[:, D:] = dv_acc[:rows].astype(BF)
    kg = None
    for p in range(3):
        f = jnp.sum((dk_acc[p*rows:(p+1)*rows] * kv[p][:, :D].astype(F32)).reshape(-1, 8, D), axis=0)
        kg = f if kg is None else kg + f
    kgain_ref[...] += kg

def attn(par, lo, gq, q, g, own, h1a, h1b, h2, off, hc, qg_prev=None):
    rows = q.shape[0]; T = 128
    win = 2*rows + T
    kvs = pl.BlockSpec((rows, 2*D), lambda h: (0, h))
    qs = pl.BlockSpec((rows, 2*D), lambda h: (0, off+h))
    in_specs=[pl.BlockSpec(memory_space=pltpu.SMEM),
              pl.BlockSpec((1,rows), lambda h:(0,0)),
              pl.BlockSpec((D,1), lambda h:(0,0)),
              qs, qs, kvs,kvs,kvs,kvs]
    args=[par,lo,gq,q,g,own,h1a,h1b,h2]
    body = functools.partial(attn_body, T, rows)
    alias={}
    if qg_prev is not None:
        in_specs.append(pl.BlockSpec(memory_space=pl.ANY)); args.append(qg_prev); alias={9:0}
        inner = body
        body = lambda *r: inner(*r[:9], *r[10:])
    return pl.pallas_call(body, grid=(hc,), in_specs=in_specs,
        out_specs=[qs, kvs,kvs,kvs,
                   pl.BlockSpec((D,2*T), lambda h:(0,0)), pl.BlockSpec((8,D), lambda h:(0,0))],
        out_shape=[jax.ShapeDtypeStruct(q.shape,BF), jax.ShapeDtypeStruct((rows,hc*2*D),F32),
                   jax.ShapeDtypeStruct((rows,hc*2*D),BF), jax.ShapeDtypeStruct((rows,hc*2*D),BF),
                   jax.ShapeDtypeStruct((D,2*T),F32), jax.ShapeDtypeStruct((8,D),F32)],
        scratch_shapes=[pltpu.VMEM((rows,2*D),BF),pltpu.VMEM((D,3*rows),BF),
            pltpu.VMEM((2,win,2*T),F32),pltpu.VMEM((2,win,2*T),F32),pltpu.VMEM((16,128),BF),pltpu.VMEM((2,win,2*T),BF),
            pltpu.VMEM((3*rows,D),F32),pltpu.VMEM((3*rows,D),F32)],
        input_output_aliases=alias,
        cost_estimate=pl.CostEstimate(flops=hc*6*10**9, bytes_accessed=hc*rows*D*24, transcendentals=0),
        compiler_params=pltpu.CompilerParams(dimension_semantics=("arbitrary",), vmem_limit_bytes=60*1024*1024),
        name="attn_grad")(*args)


def pack_body(chunks, k_ref, v_ref, gain_ref, *outs):
    h = pl.program_id(0)
    k = k_ref[...].astype(F32)
    inv = lax.rsqrt(jnp.mean(k*k, axis=1, keepdims=True) + EPS)
    k = (k * inv * gain_ref[...]).astype(BF)
    at = 0
    for hc, out in zip(chunks, outs):
        @pl.when((h >= at) & (h < at + hc))
        def _(out=out):
            out[:, :D] = k
            out[:, D:] = v_ref[...]
        at += hc


def pack(k_raw, values, k_gain, off, chunks):
    rows = k_raw.shape[0]
    cb = [pl.BlockSpec((rows, D), lambda h: (0, off + h))] * 2
    outs, at = [], 0
    for hc in chunks:
        outs.append(pl.BlockSpec((rows, 2*D), lambda h, at=at, hc=hc: (0, jnp.clip(h - at, 0, hc - 1))))
        at += hc
    return pl.pallas_call(
        functools.partial(pack_body, chunks), grid=(at,),
        in_specs=cb + [pl.BlockSpec((1, D), lambda h: (0, 0))],
        out_specs=outs,
        out_shape=[jax.ShapeDtypeStruct((rows, hc*2*D), BF) for hc in chunks],
        cost_estimate=pl.CostEstimate(flops=at*10**9, bytes_accessed=at*rows*D*8, transcendentals=0),
        name="pack_kv")(k_raw, values, k_gain)


def finish_body(par_ref, own_ref, x_ref, y_ref, k_ref, gain_ref, *refs):
    kg_ref, vg_ref = refs[-2:]
    even = jnp.where(par_ref[0] == 0, 1.0, 0.0)
    t = own_ref[...] + y_ref[...].astype(F32) + x_ref[...].astype(F32) * even
    vg_ref[...] = t[:, D:].astype(BF)
    k = k_ref[...].astype(F32)
    inv = lax.rsqrt(jnp.mean(k*k, axis=1, keepdims=True) + EPS)
    unit = k * inv
    up = t[:, :D] * gain_ref[...]
    kg_ref[...] = (inv * (up - unit * jnp.mean(up * unit, axis=1, keepdims=True))).astype(BF)


def finish(par, own, x, y, k_raw, k_gain, off, hc, prev):
    rows = own.shape[0]
    kvs = pl.BlockSpec((rows, 2*D), lambda h: (0, h))
    cb = pl.BlockSpec((rows, D), lambda h: (0, off + h))
    in_specs = [pl.BlockSpec(memory_space=pltpu.SMEM), kvs, kvs, kvs, cb, pl.BlockSpec((1, D), lambda h: (0, 0))]
    args = [par, own, x, y, k_raw, k_gain]
    alias = {}
    if prev is not None:
        in_specs += [pl.BlockSpec(memory_space=pl.ANY)] * 2
        args += list(prev)
        alias = {6: 0, 7: 1}
    return pl.pallas_call(
        finish_body, grid=(hc,), in_specs=in_specs, out_specs=[cb, cb],
        out_shape=[jax.ShapeDtypeStruct(k_raw.shape, BF)] * 2,
        cost_estimate=pl.CostEstimate(flops=hc*10**9, bytes_accessed=hc*rows*D*8, transcendentals=0),
        input_output_aliases=alias, name="finish_kv")(*args)


def move(value, pairs, name):
    with jax.named_scope(name):
        return lax.ppermute(value, "ctx", pairs)


def after(value, *others):
    return lax.optimization_barrier((value, others))[0]


def sum_over(x, name):
    count = lax.axis_size(name)
    if count & (count - 1):
        return lax.psum(x, name)
    step = 1
    while step < count:
        x = x + lax.ppermute(x, name, [(i, i ^ step) for i in range(count)])
        step *= 2
    return x


def on_device(q_raw, k_raw, values, d_out, doc_ids, q_gain, k_gain):
    rows = q_raw.shape[0]
    kv_local = k_raw.shape[1] // D
    count = lax.axis_size("ctx")
    assert 2 * rows == W and count % 2 == 0 and q_raw.shape[1] == 2 * k_raw.shape[1]
    chunks = CHUNKS if kv_local == sum(CHUNKS) else (1,) * kv_local
    factor = QUERY_SCALE ** (-0.5)
    me = lax.axis_index("ctx")
    par = (me % 2).astype(jnp.int32).reshape(1)
    onward = [(i, i + 2) for i in range(count - 2)]
    back = [(i + 2, i) for i in range(count - 2)]
    swap = [(i, i ^ 1) for i in range(count)]
    up = [(i, i + 1) for i in range(0, count, 2)]
    down = [(i + 1, i) for i in range(0, count, 2)]

    gk = k_gain.reshape(1, D)
    n = len(chunks)
    own = list(pack(k_raw, values, gk, 0, chunks[:1])) + list(pack(k_raw, values, gk, chunks[0], chunks[1:]))
    far, near_a, near_b = [None] * n, [None] * n, [None] * n
    for c in range(n):
        far[c] = move(own[c], onward, f"far{c}")
        near_a[c] = move(own[c], up, f"up{c}")

    def relay(c):
        near_b[c] = move(far[c], down, f"relay{c}")

    for c in range(min(EARLY, n)):
        relay(c)

    padded = jnp.concatenate([jnp.full((W,), -1, jnp.int32), doc_ids])
    span_ids = lax.dynamic_slice_in_dim(padded, me * rows, W + rows)
    q_ids = span_ids[W:]
    first = jnp.sum((span_ids[:, None] < q_ids[None, :]).astype(jnp.int32), axis=0)
    lo = jnp.maximum(first, jnp.arange(1, rows + 1, dtype=jnp.int32)).reshape(1, rows)
    gq = (q_gain * factor).reshape(D, 1)

    offs = [sum(chunks[:c]) for c in range(n)]
    qg = None
    mine, r1, r2, qs, kss, xs, ys = [], [], [], [], [], [], []

    def give(c, last):
        t = after(r2[c], last)
        both = (t.astype(F32) + xs[c].astype(F32)).astype(BF)
        t = jnp.where(par[0] == 1, both, t)
        ys.append(move(t, back, f"ret{c}"))
        return t

    tok = par
    for c in range(n):
        if c + 1 >= EARLY and c + 1 < n:
            if c:
                far[c + 1] = after(far[c + 1], kss[c - 1])
            relay(c + 1)
        if c + 1 < EARLY and 0 < c < n - 1:
            tok, near_b[c + 1] = lax.optimization_barrier((tok, near_b[c + 1]))
        if c >= 2:
            tok = after(tok, give(c - 2, kss[c - 1]))
        if c >= 3:
            tok, ys[c - 3] = lax.optimization_barrier((tok, ys[c - 3]))
        qg, o, a, b, s, t = attn(tok, lo, gq, q_raw, d_out, own[c], near_a[c], near_b[c], far[c], offs[c], chunks[c], qg)
        mine.append(o); r1.append(a); r2.append(b); qs.append(s); kss.append(t)
        xs.append(move(r1[c], swap, f"swap{c}"))
    out = None
    give(n - 2, kss[n - 1])
    for c in range(n - 2):
        out = finish(after(par, ys[n - 2] if False else kss[n - 1]), mine[c], xs[c], ys[c], k_raw, gk, offs[c], chunks[c], out)
    t = give(n - 1, out[0])
    out = finish(after(par, t), mine[n - 2], xs[n - 2], ys[n - 2], k_raw, gk, offs[n - 2], chunks[n - 2], out)
    q_part = jnp.sum(sum(qs), axis=1) * factor
    k_part = jnp.sum(sum(kss), axis=0) / k_gain
    gains = after(jnp.stack([q_part, k_part]), t, out[0] if GATE2 else t)
    gains = sum_over(sum_over(gains, "head"), "ctx")
    out = finish(par, mine[n - 1], xs[n - 1], ys[n - 1], k_raw, gk, offs[n - 1], chunks[n - 1], out)
    total = rows * count
    return (qg, out[0], out[1], gains[0] / math.sqrt(total * Q_HEADS), gains[1] / math.sqrt(total * KV_HEADS))


def solution(mesh):
    split = P("ctx", "head")
    return jax.shard_map(
        on_device,
        mesh=mesh,
        in_specs=(split, split, split, split, P(), P(), P()),
        out_specs=(split, split, split, P(), P()),
        check_vma=False,
    )
```

```python
import functools
import math

import jax
import jax.numpy as jnp
from jax import lax
from jax.experimental import pallas as pl
from jax.experimental.pallas import tpu as pltpu
from jax.sharding import PartitionSpec as P

Q_HEADS = 32
KV_HEADS = 16
W = 1024
QUERY_SCALE = 168
EPS = 1e-06
CHUNKS = (2, 3, 2, 1)
GATE = 1
GATE2 = 0
EARLY = 2
DIRECT = 0
D=128
BF=jnp.bfloat16
F32=jnp.float32
NT=(((1,),(1,)),((),()))
NN=(((1,),(0,)),((),()))
ORDER="half"
ACC="rmw"
def dotf(a,b,dims):
    return lax.dot_general(a,b,dims,preferred_element_type=F32)

def attn_body(T, rows, par_ref, lo_ref, gq_ref, q_ref, g_ref, own_ref, h1a_ref, h1b_ref, h2_ref,
              qg_ref, own_out, r1_out, r2_out, qgain_ref, kgain_ref,
              near, kt, s_s, dp_s, w_s, ds_s, dk_acc, dv_acc):
    h = pl.program_id(0)
    nq = rows // T
    nb = 2 * nq + 1
    @pl.when(par_ref[0] == 1)
    def _(): near[...] = h1a_ref[...]
    @pl.when(par_ref[0] == 0)
    def _(): near[...] = h1b_ref[...]
    @pl.when(h == 0)
    def _():
        qgain_ref[...] = jnp.zeros_like(qgain_ref); kgain_ref[...] = jnp.zeros_like(kgain_ref)
    kv = [h2_ref, near, own_ref]
    def kk(j): return kv[j//nq][(j%nq)*T:(j%nq+1)*T, :D]
    def vv(j): return kv[j//nq][(j%nq)*T:(j%nq+1)*T, D:]
    for p in range(3):
        kt[:, p*rows:(p+1)*rows] = kv[p][:, :D].T
    gq = gq_ref[...]
    iota = lax.broadcasted_iota(jnp.int32, (T, 2*T), 0)
    lane = lax.broadcasted_iota(jnp.int32, (T, 2*T), 1)
    tok = jnp.where(lane >= T, lane - T, lane)
    def fold(x, op):
        return op(x.reshape(T//8, 8, 2*T), axis=0)
    st = [dict() for _ in range(nq)]
    def sl(kb): return slice(kb*T, (kb+1)*T)
    def p0(i):
        t = st[i]
        r = slice(i*T, (i+1)*T)
        qf = jnp.concatenate([q_ref[r, :D].T, q_ref[r, D:].T], axis=1).astype(F32)
        t["inv"] = lax.rsqrt(jnp.mean(qf*qf, axis=0, keepdims=True) + 1e-6)
        unit = qf * t["inv"]
        t["unit"] = unit
        t["qt"] = (unit * gq).astype(BF)
        t["gt"] = jnp.concatenate([g_ref[r, :D].T, g_ref[r, D:].T], axis=1)
        lo = lo_ref[:, r] - i*T
        t["lo"] = jnp.concatenate([lo, lo], axis=1)
        yield
    def p1(i):
        t = st[i]; b = i % 2; m8 = None
        for kb in range(nb):
            s = dotf(kk(i+kb), t["qt"], NN)
            see = iota >= t["lo"] - kb*T
            if kb == nb-1: see = see & (iota <= tok)
            s = jnp.where(see, s, -1e30)
            s_s[b, sl(kb)] = s
            f = fold(s, jnp.max)
            m8 = f if m8 is None else jnp.maximum(m8, f)
            yield
        t["m"] = jnp.max(m8, axis=0, keepdims=True)
    def p2(i):
        t = st[i]; b = i % 2; l8 = None
        for kb in range(nb):
            e = jnp.exp(s_s[b, sl(kb)] - t["m"])
            s_s[b, sl(kb)] = e
            f = fold(e, jnp.sum)
            l8 = f if l8 is None else l8 + f
            dp_s[b, sl(kb)] = dotf(vv(i+kb), t["gt"], NN)
            yield
        t["il"] = 1.0 / jnp.sum(l8, axis=0, keepdims=True)
    def acc(ref, first, j, val):
        r = slice(j*T, (j+1)*T)
        if first: ref[r] = val
        else: ref[r] = ref[r] + val
    def p3(i):
        t = st[i]; b = i % 2; d8 = None
        for kb in range(nb):
            w = (s_s[b, sl(kb)] * t["il"]).astype(BF)
            f = fold(w.astype(F32) * dp_s[b, sl(kb)], jnp.sum)
            d8 = f if d8 is None else d8 + f
            if ACC == "rmw":
                acc(dv_acc, i == 0 or kb == nb-1, i+kb, dotf(w, t["gt"], NT))
            yield
        t["delta"] = jnp.sum(d8, axis=0, keepdims=True)
    def p4(i):
        t = st[i]; b = i % 2
        for kb in range(nb):
            p = s_s[b, sl(kb)] * t["il"]
            ds = (p * (dp_s[b, sl(kb)] - t["delta"])).astype(BF)
            ds_s[b, sl(kb)] = ds
            acc(dk_acc, i == 0 or kb == nb-1, i+kb, dotf(ds, t["qt"], NT))
            yield
    def p5(i):
        t = st[i]; b = i % 2
        dq = dotf(kt[:, i*T:(i+nb)*T], ds_s[b], NN)
        qgain_ref[...] += dq * t["unit"]
        up = dq * gq
        mean = jnp.mean(up * t["unit"], axis=0, keepdims=True)
        qr = (t["inv"] * (up - t["unit"] * mean)).astype(BF)
        r = slice(i*T, (i+1)*T)
        qg_ref[r, :D] = qr[:, :T].T
        qg_ref[r, D:] = qr[:, T:].T
        yield
    def run(*gens):
        gens = list(gens)
        while gens:
            for g in list(gens):
                try: next(g)
                except StopIteration: gens.remove(g)
    def chain(*gs):
        for g in gs: yield from g
    if ORDER == "seq":
        for i in range(nq):
            run(chain(p0(i), p1(i), p2(i), p3(i), p4(i), p5(i)))
    elif ORDER == "half":
        run(chain(p0(0), p1(0), p2(0)))
        for i in range(nq):
            nxt = [chain(p0(i+1), p1(i+1), p2(i+1))] if i+1 < nq else []
            run(chain(p3(i), p4(i), p5(i)), *nxt)
    elif ORDER == "pair":
        for i in range(0, nq, 2):
            run(chain(p0(i), p1(i), p2(i), p3(i), p4(i), p5(i)), chain(p0(i+1), p1(i+1), p2(i+1), p3(i+1), p4(i+1), p5(i+1)))
    own_out[:, :D] = dk_acc[2*rows:]; own_out[:, D:] = dv_acc[2*rows:]
    r1_out[:, :D] = dk_acc[rows:2*rows].astype(BF); r1_out[:, D:] = dv_acc[rows:2*rows].astype(BF)
    r2_out[:, :D] = dk_acc[:rows].astype(BF); r2_out[:, D:] = dv_acc[:rows].astype(BF)
    kg = None
    for p in range(3):
        f = jnp.sum((dk_acc[p*rows:(p+1)*rows] * kv[p][:, :D].astype(F32)).reshape(-1, 8, D), axis=0)
        kg = f if kg is None else kg + f
    kgain_ref[...] += kg

def attn(par, lo, gq, q, g, own, h1a, h1b, h2, off, hc, qg_prev=None):
    rows = q.shape[0]; T = 128
    win = 2*rows + T
    kvs = pl.BlockSpec((rows, 2*D), lambda h: (0, h))
    qs = pl.BlockSpec((rows, 2*D), lambda h: (0, off+h))
    in_specs=[pl.BlockSpec(memory_space=pltpu.SMEM),
              pl.BlockSpec((1,rows), lambda h:(0,0)),
              pl.BlockSpec((D,1), lambda h:(0,0)),
              qs, qs, kvs,kvs,kvs,kvs]
    args=[par,lo,gq,q,g,own,h1a,h1b,h2]
    body = functools.partial(attn_body, T, rows)
    alias={}
    if qg_prev is not None:
        in_specs.append(pl.BlockSpec(memory_space=pl.ANY)); args.append(qg_prev); alias={9:0}
        inner = body
        body = lambda *r: inner(*r[:9], *r[10:])
    return pl.pallas_call(body, grid=(hc,), in_specs=in_specs,
        out_specs=[qs, kvs,kvs,kvs,
                   pl.BlockSpec((D,2*T), lambda h:(0,0)), pl.BlockSpec((8,D), lambda h:(0,0))],
        out_shape=[jax.ShapeDtypeStruct(q.shape,BF), jax.ShapeDtypeStruct((rows,hc*2*D),F32),
                   jax.ShapeDtypeStruct((rows,hc*2*D),BF), jax.ShapeDtypeStruct((rows,hc*2*D),BF),
                   jax.ShapeDtypeStruct((D,2*T),F32), jax.ShapeDtypeStruct((8,D),F32)],
        scratch_shapes=[pltpu.VMEM((rows,2*D),BF),pltpu.VMEM((D,3*rows),BF),
            pltpu.VMEM((2,win,2*T),F32),pltpu.VMEM((2,win,2*T),F32),pltpu.VMEM((16,128),BF),pltpu.VMEM((2,win,2*T),BF),
            pltpu.VMEM((3*rows,D),F32),pltpu.VMEM((3*rows,D),F32)],
        input_output_aliases=alias,
        cost_estimate=pl.CostEstimate(flops=hc*6*10**9, bytes_accessed=hc*rows*D*24, transcendentals=0),
        compiler_params=pltpu.CompilerParams(dimension_semantics=("arbitrary",), vmem_limit_bytes=60*1024*1024),
        name="attn_grad")(*args)


def pack_body(chunks, k_ref, v_ref, gain_ref, *outs):
    h = pl.program_id(0)
    k = k_ref[...].astype(F32)
    inv = lax.rsqrt(jnp.mean(k*k, axis=1, keepdims=True) + EPS)
    k = (k * inv * gain_ref[...]).astype(BF)
    at = 0
    for hc, out in zip(chunks, outs):
        @pl.when((h >= at) & (h < at + hc))
        def _(out=out):
            out[:, :D] = k
            out[:, D:] = v_ref[...]
        at += hc


def pack(k_raw, values, k_gain, off, chunks):
    rows = k_raw.shape[0]
    cb = [pl.BlockSpec((rows, D), lambda h: (0, off + h))] * 2
    outs, at = [], 0
    for hc in chunks:
        outs.append(pl.BlockSpec((rows, 2*D), lambda h, at=at, hc=hc: (0, jnp.clip(h - at, 0, hc - 1))))
        at += hc
    return pl.pallas_call(
        functools.partial(pack_body, chunks), grid=(at,),
        in_specs=cb + [pl.BlockSpec((1, D), lambda h: (0, 0))],
        out_specs=outs,
        out_shape=[jax.ShapeDtypeStruct((rows, hc*2*D), BF) for hc in chunks],
        cost_estimate=pl.CostEstimate(flops=at*10**9, bytes_accessed=at*rows*D*8, transcendentals=0),
        name="pack_kv")(k_raw, values, k_gain)


def finish_body(par_ref, own_ref, x_ref, y_ref, k_ref, gain_ref, *refs):
    kg_ref, vg_ref = refs[-2:]
    even = jnp.where(par_ref[0] == 0, 1.0, 0.0)
    t = own_ref[...] + y_ref[...].astype(F32) + x_ref[...].astype(F32) * even
    vg_ref[...] = t[:, D:].astype(BF)
    k = k_ref[...].astype(F32)
    inv = lax.rsqrt(jnp.mean(k*k, axis=1, keepdims=True) + EPS)
    unit = k * inv
    up = t[:, :D] * gain_ref[...]
    kg_ref[...] = (inv * (up - unit * jnp.mean(up * unit, axis=1, keepdims=True))).astype(BF)


def finish(par, own, x, y, k_raw, k_gain, off, hc, prev):
    rows = own.shape[0]
    kvs = pl.BlockSpec((rows, 2*D), lambda h: (0, h))
    cb = pl.BlockSpec((rows, D), lambda h: (0, off + h))
    in_specs = [pl.BlockSpec(memory_space=pltpu.SMEM), kvs, kvs, kvs, cb, pl.BlockSpec((1, D), lambda h: (0, 0))]
    args = [par, own, x, y, k_raw, k_gain]
    alias = {}
    if prev is not None:
        in_specs += [pl.BlockSpec(memory_space=pl.ANY)] * 2
        args += list(prev)
        alias = {6: 0, 7: 1}
    return pl.pallas_call(
        finish_body, grid=(hc,), in_specs=in_specs, out_specs=[cb, cb],
        out_shape=[jax.ShapeDtypeStruct(k_raw.shape, BF)] * 2,
        cost_estimate=pl.CostEstimate(flops=hc*10**9, bytes_accessed=hc*rows*D*8, transcendentals=0),
        input_output_aliases=alias, name="finish_kv")(*args)


def move(value, pairs, name):
    with jax.named_scope(name):
        return lax.ppermute(value, "ctx", pairs)


def after(value, *others):
    return lax.optimization_barrier((value, others))[0]


def sum_over(x, name):
    count = lax.axis_size(name)
    if count & (count - 1):
        return lax.psum(x, name)
    step = 1
    while step < count:
        x = x + lax.ppermute(x, name, [(i, i ^ step) for i in range(count)])
        step *= 2
    return x


def on_device(q_raw, k_raw, values, d_out, doc_ids, q_gain, k_gain):
    rows = q_raw.shape[0]
    kv_local = k_raw.shape[1] // D
    count = lax.axis_size("ctx")
    assert 2 * rows == W and count % 2 == 0 and q_raw.shape[1] == 2 * k_raw.shape[1]
    chunks = CHUNKS if kv_local == sum(CHUNKS) else (1,) * kv_local
    factor = QUERY_SCALE ** (-0.5)
    me = lax.axis_index("ctx")
    par = (me % 2).astype(jnp.int32).reshape(1)
    onward = [(i, i + 2) for i in range(count - 2)]
    back = [(i + 2, i) for i in range(count - 2)]
    swap = [(i, i ^ 1) for i in range(count)]
    up = [(i, i + 1) for i in range(0, count, 2)]
    down = [(i + 1, i) for i in range(0, count, 2)]

    gk = k_gain.reshape(1, D)
    n = len(chunks)
    own = list(pack(k_raw, values, gk, 0, chunks[:1])) + list(pack(k_raw, values, gk, chunks[0], chunks[1:]))
    far, near_a, near_b = [None] * n, [None] * n, [None] * n
    for c in range(n):
        far[c] = move(own[c], onward, f"far{c}")
        near_a[c] = move(own[c], up, f"up{c}")

    def relay(c):
        near_b[c] = move(far[c], down, f"relay{c}")

    for c in range(min(EARLY, n)):
        relay(c)

    padded = jnp.concatenate([jnp.full((W,), -1, jnp.int32), doc_ids])
    span_ids = lax.dynamic_slice_in_dim(padded, me * rows, W + rows)
    q_ids = span_ids[W:]
    first = jnp.sum((span_ids[:, None] < q_ids[None, :]).astype(jnp.int32), axis=0)
    lo = jnp.maximum(first, jnp.arange(1, rows + 1, dtype=jnp.int32)).reshape(1, rows)
    gq = (q_gain * factor).reshape(D, 1)

    offs = [sum(chunks[:c]) for c in range(n)]
    qg = None
    mine, r1, r2, qs, kss, xs, ys = [], [], [], [], [], [], []

    def give(c, last):
        t = after(r2[c], last)
        both = (t.astype(F32) + xs[c].astype(F32)).astype(BF)
        t = jnp.where(par[0] == 1, both, t)
        ys.append(move(t, back, f"ret{c}"))
        return t

    tok = par
    for c in range(n):
        if c + 1 >= EARLY and c + 1 < n:
            if c:
                far[c + 1] = after(far[c + 1], kss[c - 1])
            relay(c + 1)
        if c + 1 < EARLY and 0 < c < n - 1:
            tok, near_b[c + 1] = lax.optimization_barrier((tok, near_b[c + 1]))
        if c >= 2:
            tok = after(tok, give(c - 2, kss[c - 1]))
        if c >= 3:
            tok, ys[c - 3] = lax.optimization_barrier((tok, ys[c - 3]))
        qg, o, a, b, s, t = attn(tok, lo, gq, q_raw, d_out, own[c], near_a[c], near_b[c], far[c], offs[c], chunks[c], qg)
        mine.append(o); r1.append(a); r2.append(b); qs.append(s); kss.append(t)
        xs.append(move(r1[c], swap, f"swap{c}"))
    out = None
    give(n - 2, kss[n - 1])
    for c in range(n - 2):
        out = finish(after(par, ys[n - 2] if False else kss[n - 1]), mine[c], xs[c], ys[c], k_raw, gk, offs[c], chunks[c], out)
    t = give(n - 1, out[0])
    out = finish(after(par, t), mine[n - 2], xs[n - 2], ys[n - 2], k_raw, gk, offs[n - 2], chunks[n - 2], out)
    q_part = jnp.sum(sum(qs), axis=1) * factor
    k_part = jnp.sum(sum(kss), axis=0) / k_gain
    gains = after(jnp.stack([q_part, k_part]), t, out[0] if GATE2 else t)
    gains = sum_over(sum_over(gains, "head"), "ctx")
    out = finish(par, mine[n - 1], xs[n - 1], ys[n - 1], k_raw, gk, offs[n - 1], chunks[n - 1], out)
    total = rows * count
    return (qg, out[0], out[1], gains[0] / math.sqrt(total * Q_HEADS), gains[1] / math.sqrt(total * KV_HEADS))


def solution(mesh):
    split = P("ctx", "head")
    return jax.shard_map(
        on_device,
        mesh=mesh,
        in_specs=(split, split, split, split, P(), P(), P()),
        out_specs=(split, split, split, P(), P()),
        check_vma=False,
    )
```
